32 devices in a mesh: grp: 2 (over x), ep: 8 (over z, y), sub: 2 (over core).
Axes of the slice: x: 2, y: 2, z: 4, core: 2. Of those that a mesh axis runs over, the one named last changes fastest.
Arguments:
- queries: bfloat16 [320, 16, 128], P(('grp', 'ep'), 'sub'), parts along dimension 0
- cache_keys: bfloat16 [320, 2, 384, 128], P(('grp', 'ep'), 'sub'), parts along dimension 0, may hold values from -6 to 6
- cache_values: bfloat16 [320, 2, 384, 128], P(('grp', 'ep'), 'sub'), parts along dimension 0, may hold values from -6 to 6
- new_keys: bfloat16 [320, 2, 128], P(('grp', 'ep'), 'sub'), parts along dimension 0
- new_values: bfloat16 [320, 2, 128], P(('grp', 'ep'), 'sub'), parts along dimension 0, may hold values from -6 to 6
- lengths: int32 [320], P(('grp', 'ep')), parts along dimension 0, may hold values from 1 to 384, as said below
- out_proj: bfloat16 [2048, 2048], P('sub'), may hold values from -1.5 to 1.5
- residual: bfloat16 [320, 2048], P(('grp', 'ep', 'sub')), parts along dimension 0, may hold values from -6 to 6
- norm_gain: float32 [2048], replicated, may hold values from 0.25 to 1.75
- gate_proj: bfloat16 [64, 2048, 768], P(('ep', 'sub')), may hold values from -0.125 to 0.125
- up_proj: bfloat16 [64, 2048, 768], P(('ep', 'sub')), may hold values from -0.125 to 0.125
- down_proj: bfloat16 [64, 768, 2048], P(('ep', 'sub')), may hold values from -0.21875 to 0.21875
- routing: int32 [320, 8], P(('grp', 'ep', 'sub')), parts along dimension 0, may hold values from 0 to 63, all different within a row; in each aligned block of 10 rows (0 to 9, 10 to 19, ...) at most 3 rows name the same one
- route_weights: float32 [320, 8], P(('grp', 'ep', 'sub')), parts along dimension 0, may hold values from 0.05 to 1
Outputs:
- layer_out: bfloat16 [320, 2048], P(('grp', 'ep', 'sub')), parts along dimension 0
The draws below stay inside these ranges and needn't reach their ends.
There are 2 independent parts, one for each index of `grp`. The reference program is written for one: setup_inputs(seed, part) draws one part's arguments, and reference() takes and returns one part's arrays. A program takes and returns all parts, laid end to end along the dimension named above; an argument that names none is the same for every part. Nothing has to cross between parts.
Inputs may be any that keep to these rules, and one draw needn't show every extreme that they name: Slots 0 to lengths - 1 of a request are live; some request has exactly 384. `routing`: each request names 8 different experts; among the 10 requests of one device no expert is named by more than 3, and some device reaches 3.
All inputs are finite; a program needn't handle non-finite values.
Results may differ from the reference program's by a relative error of at most 0.007.
Values may be sent and summed in bfloat16 or wider, within the bound.
A program may use at most 128 MiB of HBM per device.

```python
import math
import jax
import jax.numpy as jnp
import numpy as np
from jax import lax

D = 2048
HD = 128
FF = 768
TOP = 8
HQ = 16
KVH = 2
EXPERTS = 64
WIN = 384
ROWS_DEV = 10
MOST = 3
ROWS = 160


def common_keys(key):
    base = jax.random.fold_in(key, 11)
    return jax.random.truncated_normal(base, -6.0, 6.0, (ROWS, KVH, WIN, HD), jnp.float32)


def draw_cache_keys(key, part):
    return common_keys(key).astype(jnp.bfloat16)


def draw_queries(key, part):
    values = jax.random.truncated_normal(jax.random.fold_in(key, 12), -6.0, 6.0, (ROWS, HQ, HD), jnp.float32)
    return values.astype(jnp.bfloat16)


def draw_new_keys(key, part):
    values = jax.random.truncated_normal(jax.random.fold_in(key, 13), -6.0, 6.0, (ROWS, KVH, HD), jnp.float32)
    return values.astype(jnp.bfloat16)


def draw_lengths(key, part):
    values = jax.random.randint(jax.random.fold_in(key, 14), (ROWS,), 1, WIN + 1, jnp.int32)
    return values.at[0].set(WIN)


def block_levels(stream_key, extent, shards, smallest, high):
    level, own = 1.0, jax.random.fold_in(stream_key, 6)
    for dim, parts in shards:
        heights = jnp.exp(jax.random.uniform(jax.random.fold_in(own, dim), (parts,), jnp.float32, smallest / len(shards), high / len(shards)))
        level = level * jnp.repeat(heights, extent[dim] // parts).reshape([-1 if axis == dim else 1 for axis in range(len(extent))])
    return level


def assign_block(rng, own, number, rows, number_of, top, bound, slope):
    sequence = jax.random.permutation(rng, number_of)
    packed, ordinary = portions_of(number_of, rows * top, bound, slope, True), portions_of(number_of, rows * top, bound, slope, False)
    places = jnp.arange(number_of)

    def named(tallies, rotation):
        used = int((tallies > 0).sum())
        fixed = max(1, used // 4)
        moved = fixed + (places - fixed + rotation * (used - fixed)) % max(1, number_of - fixed)
        return jnp.zeros((number_of,), jnp.int32).at[sequence[jnp.where(places < fixed, places, moved)]].set(jnp.asarray(tallies, jnp.int32))

    tallies = jnp.where(number % 4 == 0, named(packed, number // 4), named(ordinary, number - number // 4 - 1))
    mixed = jax.random.permutation(jax.random.fold_in(own, 3), number_of)
    source_of, taker = mixed[0:number_of // 2 * 2:2], mixed[1:number_of // 2 * 2:2]
    margin = jnp.minimum(tallies[source_of] - 1, bound - tallies[taker]) // 2
    margin = jnp.where((source_of == sequence[0]) | (taker == sequence[0]) | (tallies[taker] == 0), 0, jnp.maximum(margin, 0))
    moved = jax.random.randint(jax.random.fold_in(own, 4), (number_of // 2,), 0, 1 << 20) % (margin + 1)
    tallies = tallies.at[source_of].add(-moved).at[taker].add(moved)
    items = jnp.searchsorted(jnp.cumsum(tallies), jnp.arange(rows * top), side="right").astype(jnp.int32)
    table = items.reshape(top, rows).T
    table = table[jax.random.permutation(jax.random.fold_in(own, 1), rows)]
    rotation = jax.random.randint(jax.random.fold_in(own, 2), (rows, 1), 0, top)
    return jnp.take_along_axis(table, (jnp.arange(top)[None, :] + rotation) % top, axis=1)


def portions_of(count, total, reach, skew, full):
    weights = [(1 << 20) // math.isqrt(grade ** skew) + 1 for grade in range(1, count + 1)]
    largest = reach if full else min(reach, max(-(-total // count), total * weights[0] // sum(weights)))
    least = 1 if total - largest >= count - 1 else 0
    given, surplus = [largest] + [least] * (count - 1), total - largest - least * (count - 1)
    while surplus > 0:
        candidates = [i for i in range(1, count) if given[i] < largest] or [i for i in range(1, count) if given[i] < reach]
        whole, budget = sum([weights[i] for i in candidates]), surplus
        for i in candidates:
            more = min(reach - given[i], max(1, budget * weights[i] // whole), surplus)
            given[i] = given[i] + more
            surplus = surplus - more
    return np.array(given)


def centred(stream_key, extent, spread, most, split=(), held_as=jnp.bfloat16):
    result = spread * jax.random.normal(stream_key, extent, jnp.float32)
    if split:
        result = result * block_levels(stream_key, extent, split, -0.22, 0.18)
    return jnp.clip(result, -most, most).astype(held_as)


def setup_inputs(seed: int = 0, part: int = 0) -> dict:
    key_list = jax.random.split(jax.random.key(seed), 15)
    part_keys = jax.random.split(jax.random.fold_in(key_list[14], part), 15)
    queries = draw_queries(jax.random.fold_in(jax.random.fold_in(key_list[14], part), 71), part)
    cache_keys = draw_cache_keys(jax.random.fold_in(jax.random.fold_in(key_list[14], part), 71), part)
    cache_values = centred(part_keys[2], (ROWS, KVH, WIN, HD), 1.0, 6.0, ((0, 8), (1, 2)))
    new_keys = draw_new_keys(jax.random.fold_in(jax.random.fold_in(key_list[14], part), 71), part)
    new_values = centred(part_keys[4], (ROWS, KVH, HD), 1.0, 6.0, ((0, 8), (1, 2)))
    lengths = draw_lengths(jax.random.fold_in(jax.random.fold_in(key_list[14], part), 71), part)
    out_proj = centred(key_list[6], (HQ * HD, D), 0.25, 1.5, ((0, 2),))
    residual = centred(part_keys[7], (ROWS, D), 1.0, 6.0, ((0, 16),))
    norm_gain = jnp.clip(1.0 + 0.15 * jax.random.normal(key_list[8], (D,), jnp.float32), 0.25, 1.75)
    gate_proj = centred(key_list[9], (EXPERTS, D, FF), D ** -0.5, 0.125, ((0, 16),))
    up_proj = centred(key_list[10], (EXPERTS, D, FF), D ** -0.5, 0.125, ((0, 16),))
    down_proj = centred(key_list[11], (EXPERTS, FF, D), FF ** -0.5, 0.21875, ((0, 16),))
    routing_keys = jax.random.split(jax.random.fold_in(part_keys[12], 1), ROWS // ROWS_DEV)
    routing_turns = jax.random.permutation(jax.random.fold_in(part_keys[12], 3), ROWS // ROWS_DEV)
    routing = jax.vmap(lambda own, number: assign_block(jax.random.fold_in(part_keys[12], 2), own, number, ROWS_DEV, EXPERTS, TOP, MOST, 2))(routing_keys, routing_turns).reshape((ROWS, TOP))
    route_weights = jnp.clip(jnp.exp(math.log(1.0) - 2.9957323 * jax.random.uniform(part_keys[13], (ROWS, TOP), jnp.float32) ** block_levels(part_keys[13], (ROWS, TOP), ((0, 16),), -0.2, 0.2)), 0.05, 1.0)
    return {"queries": queries, "cache_keys": cache_keys, "cache_values": cache_values, "new_keys": new_keys, "new_values": new_values, "lengths": lengths, "out_proj": out_proj, "residual": residual, "norm_gain": norm_gain, "gate_proj": gate_proj, "up_proj": up_proj, "down_proj": down_proj, "routing": routing, "route_weights": route_weights}


def expert_block(operands):
    inputs, gate_mat, up_mat, down_mat = operands
    gate_val = jnp.dot(inputs, gate_mat, preferred_element_type=jnp.float32)
    up_val = jnp.dot(inputs, up_mat, preferred_element_type=jnp.float32)
    hidden = (jax.nn.silu(gate_val) * up_val).astype(jnp.bfloat16)
    return jnp.dot(hidden, down_mat, preferred_element_type=jnp.float32).astype(jnp.bfloat16)

def reference(queries, cache_keys, cache_values, new_keys, new_values, lengths, out_proj, residual, norm_gain, gate_proj, up_proj, down_proj, routing, route_weights):
    group_size = HQ // KVH
    score_scale = 1.0 / math.sqrt(HD)
    grouped = queries.astype(jnp.float32).reshape(ROWS, KVH, group_size, HD)
    scores = jnp.einsum('bgqd,bgjd->bgqj', grouped, cache_keys.astype(jnp.float32)) * score_scale
    own_score = jnp.einsum('bgqd,bgd->bgq', grouped, new_keys.astype(jnp.float32)) * score_scale
    valid_mask = jnp.arange(WIN, dtype=jnp.int32)[None, :] < lengths[:, None]
    scores = jnp.where(valid_mask[:, None, None, :], scores, -1e+30)
    top_score = jnp.maximum(lax.optimization_barrier(jnp.max(scores, -1)), own_score)
    weights = jnp.exp(scores - top_score[..., None])
    own_weight = jnp.exp(own_score - top_score)
    denominator = lax.optimization_barrier(jnp.sum(weights, -1)) + own_weight
    weights_low = lax.optimization_barrier(weights.astype(jnp.bfloat16)).astype(jnp.float32)
    own_low = lax.optimization_barrier(own_weight.astype(jnp.bfloat16)).astype(jnp.float32)
    mixture = jnp.einsum('bgqj,bgjd->bgqd', weights_low, cache_values.astype(jnp.float32))
    mixture = mixture + jnp.einsum('bgq,bgd->bgqd', own_low, new_values.astype(jnp.float32))
    head_out = (mixture / denominator[..., None]).reshape(ROWS, HQ * HD).astype(jnp.bfloat16)
    stream = residual.astype(jnp.float32) + jnp.dot(head_out, out_proj, preferred_element_type=jnp.float32)
    normed = (stream * lax.rsqrt(lax.optimization_barrier(jnp.mean(stream * stream, -1, keepdims=True)) + 1e-06) * norm_gain).astype(jnp.bfloat16)
    blocks = ROWS // ROWS_DEV
    chosen = (routing[:, :, None] == jnp.arange(EXPERTS, dtype=jnp.int32)[None, None, :]).astype(jnp.int32)
    expert_hits = lax.optimization_barrier(jnp.sum(chosen, 1)).reshape(blocks, ROWS_DEV, EXPERTS)
    earlier_hits = (jnp.cumsum(expert_hits, 1) - expert_hits).reshape(ROWS, EXPERTS)
    slot_rank = jnp.take_along_axis(earlier_hits, routing, 1).astype(jnp.int32)
    block_index = (jnp.arange(ROWS, dtype=jnp.int32) // ROWS_DEV)[:, None] + jnp.zeros((ROWS, TOP), jnp.int32)
    spread_rows = jnp.broadcast_to(normed[:, None, :], (ROWS, TOP, D))
    slotted = jnp.zeros((EXPERTS, blocks, MOST, D), jnp.bfloat16).at[routing, block_index, slot_rank].set(spread_rows)
    answered = lax.map(expert_block, (slotted.reshape(EXPERTS, blocks * MOST, D), gate_proj, up_proj, down_proj))
    answered = lax.optimization_barrier(answered.reshape(EXPERTS, blocks, MOST, D))
    picked_rows = answered[routing, block_index, slot_rank].astype(jnp.float32)
    expert_sum = lax.optimization_barrier(jnp.sum(route_weights[:, :, None] * picked_rows, 1))
    return (stream + expert_sum).astype(jnp.bfloat16)
```

```python
import functools
import math

import jax
import jax.numpy as jnp
from jax import lax
from jax.experimental import pallas as pl
from jax.experimental.pallas import tpu as pltpu
from jax.sharding import PartitionSpec as P

PAD = 16
CHUNKS = 4
TILE = 256
MESH = pl.DeviceIdType.MESH
F32 = jnp.float32
BF16 = jnp.bfloat16


def kernel(
    n_ep, unroll,
    q_ref, nk_ref, nv_ref, len_ref, res_ref, gain_ref, route_ref, rw_ref,
    k_hbm, v_hbm, op_hbm, g_hbm, u_hbm, d_hbm,
    out_ref,
    k_s, v_s, op_s, g_s, u_s, d_s,
    ho, pr, prr, stream, w_own, w_all, xa, hid, part, r1, s1, r2, s2, r3,
    load_sem, g_sem, u_sem, d_sem, pr_sem, ws_sem, wr_sem,
    zs_sem, zr_sem, ys_sem, yr_sem, cs_sem, cr_sem,
    a_send, a_recv, b_send, b_recv, c_send, c_recv,
):
    nz = n_ep // 2
    n = n_ep * 2
    ep, sub = lax.axis_index("ep"), lax.axis_index("sub")
    hi, lo = ep // 2, ep % 2
    me = ep * 2 + sub
    rows, heads, hd = q_ref.shape
    half = rows // 2
    experts, width, ff = g_hbm.shape
    window = k_s.shape[1]

    def at(z, y, c):
        return {"ep": z * 2 + y, "sub": c}

    def remote(src, dst, ss, rs, where):
        return pltpu.make_async_remote_copy(
            src_ref=src, dst_ref=dst, send_sem=ss, recv_sem=rs,
            device_id=where, device_id_type=MESH,
        )

    k_cp = pltpu.make_async_copy(k_hbm, k_s, load_sem.at[0])
    v_cp = pltpu.make_async_copy(v_hbm, v_s, load_sem.at[1])
    op_cp = pltpu.make_async_copy(op_hbm, op_s, load_sem.at[2])
    k_cp.start()
    v_cp.start()
    op_cp.start()

    barrier = pltpu.get_barrier_semaphore()
    for k in range(1, n):
        peer = (me + k) % n
        pl.semaphore_signal(barrier, inc=1, device_id={"ep": peer // 2, "sub": peer % 2}, device_id_type=MESH)
    pl.semaphore_wait(barrier, n - 1)

    lanes = lax.broadcasted_iota(jnp.int32, (half, 128), 1)
    dense = jnp.zeros((half, 128), F32)
    for t in range(route_ref.shape[1]):
        dense = dense + jnp.where(route_ref[:, t : t + 1] == lanes, rw_ref[:, t : t + 1], 0.0)
    w_own[...] = jnp.zeros_like(w_own)
    w_own[0:half, :] = dense
    w_all[sub, lo, hi] = w_own[...]
    w_copies = []
    for k in range(1, n):
        peer = (me + k) % n
        cp = remote(w_own, w_all.at[sub, lo, hi], ws_sem.at[k], wr_sem.at[k], {"ep": peer // 2, "sub": peer % 2})
        cp.start()
        w_copies.append(cp)

    ho[...] = jnp.zeros_like(ho)
    k_cp.wait()
    v_cp.wait()
    for e in range(experts):
        pltpu.make_async_copy(g_hbm.at[e], g_s.at[e], g_sem.at[e]).start()
        pltpu.make_async_copy(u_hbm.at[e], u_s.at[e], u_sem.at[e]).start()
    for e in range(experts):
        pltpu.make_async_copy(d_hbm.at[e], d_s.at[e], d_sem.at[e]).start()

    scale = 1.0 / math.sqrt(hd)
    slots = lax.broadcasted_iota(jnp.int32, (heads, window), 1)

    def attend(i, carry):
        bs = [i * unroll + j for j in range(unroll)]
        qs = [q_ref[b] for b in bs]
        ss = [
            lax.dot_general(q, k_s[b], (((1,), (1,)), ((), ())), preferred_element_type=F32) * scale
            for q, b in zip(qs, bs)
        ]
        owns = [
            jnp.sum(q.astype(F32) * nk_ref[b].astype(F32), -1, keepdims=True) * scale for q, b in zip(qs, bs)
        ]
        ss = [jnp.where(slots < len_ref[b], s, -1e30) for s, b in zip(ss, bs)]
        tops = [jnp.maximum(jnp.max(s, -1, keepdims=True), o) for s, o in zip(ss, owns)]
        ws = [jnp.exp(s - t) for s, t in zip(ss, tops)]
        os = [jnp.exp(o - t) for o, t in zip(owns, tops)]
        dens = [jnp.sum(w, -1, keepdims=True) + o for w, o in zip(ws, os)]
        mixes = [
            jnp.dot(w.astype(BF16), v_s[b], preferred_element_type=F32)
            + o.astype(BF16).astype(F32) * nv_ref[b].astype(F32)
            for w, o, b in zip(ws, os, bs)
        ]
        for m, d, b in zip(mixes, dens, bs):
            ho[(b // half) * PAD + b % half] = m / d
        return carry

    lax.fori_loop(0, rows // unroll, attend, 0)

    flat = jnp.concatenate([ho[:, h, :] for h in range(heads)], axis=1).astype(BF16)
    op_cp.wait()
    piece = width // CHUNKS

    def project(j, carry):
        cols = pl.ds(pl.multiple_of(j * piece, piece), piece)
        p = jnp.dot(flat, op_s[:, cols], preferred_element_type=F32)
        pr[0, :, cols] = p[:PAD]
        pr[1, :, cols] = p[PAD:]
        return carry

    lax.fori_loop(0, CHUNKS, project, 0)
    pr_cp = remote(pr.at[1 - sub], prr, pr_sem.at[0], pr_sem.at[1], at(hi, lo, 1 - sub))
    pr_cp.start()
    pr_cp.wait()
    stream[...] = pr[sub] + prr[...]
    stream[0:half, :] = stream[0:half, :] + res_ref[...].astype(F32)
    x = stream[...]
    normed = x * lax.rsqrt(jnp.mean(x * x, -1, keepdims=True) + 1e-6) * gain_ref[...]
    xa[sub, lo, hi] = normed.astype(BF16)

    sends = []

    def go(src, ss, rs, where):
        cp = remote(src, src, ss, rs, where)
        cp.start()
        sends.append(cp)

    for k in range(1, nz):
        go(xa.at[sub, lo, hi], zs_sem.at[k], zr_sem.at[k], at((hi + k) % nz, lo, sub))
    go(xa.at[sub, lo, hi], ys_sem.at[0], yr_sem.at[0], at(hi, 1 - lo, sub))
    go(xa.at[sub, lo, hi], cs_sem.at[0, 0], cr_sem.at[0, 0], at(hi, lo, 1 - sub))

    def landed(c, y, k, rs):
        ref = xa.at[c, y, (hi - k + nz) % nz]
        remote(ref, ref, rs, rs, at(hi, lo, 1 - sub)).wait_recv()
        return ref

    for k in range(1, nz):
        ref = landed(sub, lo, k, zr_sem.at[k])
        go(ref, ys_sem.at[k], yr_sem.at[k], at(hi, 1 - lo, sub))
        go(ref, cs_sem.at[0, k], cr_sem.at[0, k], at(hi, lo, 1 - sub))
    for k in range(nz):
        ref = landed(sub, 1 - lo, k, yr_sem.at[k])
        go(ref, cs_sem.at[1, k], cr_sem.at[1, k], at(hi, lo, 1 - sub))
    for k in range(nz):
        landed(1 - sub, lo, k, cr_sem.at[0, k])
        landed(1 - sub, 1 - lo, k, cr_sem.at[1, k])
    for cp in w_copies:
        cp.wait()

    total = n * PAD
    tiles = ff // TILE
    lane = lax.broadcasted_iota(jnp.int32, (total, 128), 1)

    def expert(e, carry):
        pltpu.make_async_copy(g_hbm.at[e], g_s.at[e], g_sem.at[e]).wait()
        pltpu.make_async_copy(u_hbm.at[e], u_s.at[e], u_sem.at[e]).wait()
        w_e = jnp.sum(jnp.where(lane == me * experts + e, w_all[...].reshape(total, 128), 0.0), -1, keepdims=True)

        def tile(t, carry):
            cols = pl.ds(pl.multiple_of(t * TILE, TILE), TILE)
            xs = xa[...].reshape(total, width)
            g = jnp.dot(xs, g_s[e, :, cols], preferred_element_type=F32)
            u = jnp.dot(xs, u_s[e, :, cols], preferred_element_type=F32)
            h = (g / (1.0 + jnp.exp(-g))) * u * w_e
            hid[:, pl.ds(pl.multiple_of(e * ff + t * TILE, TILE), TILE)] = h.astype(BF16)
            return carry

        return lax.fori_loop(0, tiles, tile, carry)

    lax.fori_loop(0, experts, expert, 0)
    for e in range(experts):
        pltpu.make_async_copy(d_hbm.at[e], d_s.at[e], d_sem.at[e]).wait()

    firsts, seconds, thirds = {}, {}, {}

    def down(j):
        acc = jnp.dot(
            hid[...],
            d_s[:, :, j * piece : (j + 1) * piece].reshape(experts * ff, piece),
            preferred_element_type=F32,
        )
        part[j] = acc.astype(BF16).reshape(2, 2, nz, PAD, piece)
        firsts[j] = remote(part.at[j, 1 - sub], r1.at[j], a_send.at[j], a_recv.at[j], at(hi, lo, 1 - sub))
        firsts[j].start()

    def second(j):
        firsts[j].wait()
        s1[j] = (part[j, sub].astype(F32) + r1[j].astype(F32)).astype(BF16)
        seconds[j] = remote(s1.at[j, 1 - lo], r2.at[j], b_send.at[j], b_recv.at[j], at(hi, 1 - lo, sub))
        seconds[j].start()

    def third(j):
        seconds[j].wait()
        s2[j] = (s1[j, lo].astype(F32) + r2[j].astype(F32)).astype(BF16)
        thirds[j] = []
        for k in range(1, nz):
            z = (hi + k) % nz
            cp = remote(s2.at[j, z], r3.at[j, k], c_send.at[j, k], c_recv.at[j, k], at(z, lo, sub))
            cp.start()
            thirds[j].append(cp)

    def final(j):
        acc = s2[j, hi].astype(F32)
        for k in range(1, nz):
            thirds[j][k - 1].wait()
            acc = acc + r3[j, k].astype(F32)
        acc = acc + stream[:, j * piece : (j + 1) * piece]
        out_ref[:, j * piece : (j + 1) * piece] = acc[:half].astype(out_ref.dtype)

    for step in range(CHUNKS + 3):
        if step < CHUNKS:
            down(step)
        for lag, stage in ((1, second), (2, third), (3, final)):
            if 0 <= step - lag < CHUNKS:
                stage(step - lag)
    for cp in sends:
        cp.wait_send()


def per_device(
    queries, cache_keys, cache_values, new_keys, new_values, lengths, out_proj, residual,
    norm_gain, gate_proj, up_proj, down_proj, routing, route_weights,
):
    n_ep = lax.axis_size("ep")
    rows, heads, hd = queries.shape
    window = cache_keys.shape[2]
    half, width = residual.shape
    experts, _, ff = gate_proj.shape
    nz, n = n_ep // 2, n_ep * 2
    piece = width // CHUNKS
    unroll = next(u for u in (5, 4, 2, 1) if rows % u == 0)
    vmem = pl.BlockSpec(memory_space=pltpu.VMEM)
    hbm = pl.BlockSpec(memory_space=pl.ANY)
    dma = pltpu.SemaphoreType.DMA
    return pl.pallas_call(
        functools.partial(kernel, n_ep, unroll),
        out_shape=jax.ShapeDtypeStruct((half, width), BF16),
        in_specs=[vmem] * 3 + [pl.BlockSpec(memory_space=pltpu.SMEM)] + [vmem] * 4 + [hbm] * 6,
        out_specs=vmem,
        scratch_shapes=[
            pltpu.VMEM((rows, window, hd), BF16),
            pltpu.VMEM((rows, window, hd), BF16),
            pltpu.VMEM(out_proj.shape, BF16),
            pltpu.VMEM(gate_proj.shape, BF16),
            pltpu.VMEM(up_proj.shape, BF16),
            pltpu.VMEM(down_proj.shape, BF16),
            pltpu.VMEM((2 * PAD, heads, hd), F32),
            pltpu.VMEM((2, PAD, width), F32),
            pltpu.VMEM((PAD, width), F32),
            pltpu.VMEM((PAD, width), F32),
            pltpu.VMEM((PAD, 128), F32),
            pltpu.VMEM((2, 2, nz, PAD, 128), F32),
            pltpu.VMEM((2, 2, nz, PAD, width), BF16),
            pltpu.VMEM((n * PAD, experts * ff), BF16),
            pltpu.VMEM((CHUNKS, 2, 2, nz, PAD, piece), BF16),
            pltpu.VMEM((CHUNKS, 2, nz, PAD, piece), BF16),
            pltpu.VMEM((CHUNKS, 2, nz, PAD, piece), BF16),
            pltpu.VMEM((CHUNKS, nz, PAD, piece), BF16),
            pltpu.VMEM((CHUNKS, nz, PAD, piece), BF16),
            pltpu.VMEM((CHUNKS, nz, PAD, piece), BF16),
            dma((3,)), dma((experts,)), dma((experts,)), dma((experts,)), dma((2,)), dma((n,)), dma((n,)),
            dma((nz,)), dma((nz,)), dma((nz,)), dma((nz,)), dma((2, nz)), dma((2, nz)),
            dma((CHUNKS,)), dma((CHUNKS,)), dma((CHUNKS,)), dma((CHUNKS,)), dma((CHUNKS, nz)), dma((CHUNKS, nz)),
        ],
        compiler_params=pltpu.CompilerParams(
            collective_id=0, has_side_effects=True, vmem_limit_bytes=60 * 1024 * 1024
        ),
    )(
        queries, new_keys, new_values, lengths, residual, norm_gain.reshape(1, width), routing, route_weights,
        cache_keys.reshape(rows, window, hd), cache_values.reshape(rows, window, hd), out_proj,
        gate_proj, up_proj, down_proj,
    )


def solution(mesh):
    return jax.shard_map(
        per_device,
        mesh=mesh,
        in_specs=(
            P(("grp", "ep"), "sub", None),
            P(("grp", "ep"), "sub", None, None),
            P(("grp", "ep"), "sub", None, None),
            P(("grp", "ep"), "sub", None),
            P(("grp", "ep"), "sub", None),
            P(("grp", "ep")),
            P("sub", None),
            P(("grp", "ep", "sub"), None),
            P(),
            P(("ep", "sub"), None, None),
            P(("ep", "sub"), None, None),
            P(("ep", "sub"), None, None),
            P(("grp", "ep", "sub"), None),
            P(("grp", "ep", "sub"), None),
        ),
        out_specs=P(("grp", "ep", "sub"), None),
        check_vma=False,
    )
```

```python
import functools
import math

import jax
import jax.numpy as jnp
from jax import lax
from jax.experimental import pallas as pl
from jax.experimental.pallas import tpu as pltpu
from jax.sharding import PartitionSpec as P

PAD = 16
CHUNKS = 2
PARTS = 2
TILE = 256
MESH = pl.DeviceIdType.MESH
F32 = jnp.float32
BF16 = jnp.bfloat16


def kernel(
    n_ep, unroll,
    q_ref, nk_ref, nv_ref, len_ref, res_ref, gain_ref, route_ref, rw_ref,
    k_hbm, v_hbm, op_hbm, g_hbm, u_hbm, d_hbm,
    out_ref,
    k_s, v_s, op_s, g_s, u_s, d_s,
    ho, pr, prr, stream, w_own, w_all, w_row, nk, nv, xa, xc, hid, part, r1, s1, r2, s2, r3,
    load_sem, g_sem, u_sem, d_sem, pr_sem, ws_sem, wr_sem,
    zs_sem, zr_sem, ys_sem, yr_sem, cs_sem, cr_sem,
    a_send, a_recv, b_send, b_recv, c_send, c_recv,
):
    nz = n_ep // 2
    n = n_ep * 2
    ep, sub = lax.axis_index("ep"), lax.axis_index("sub")
    hi, lo = ep // 2, ep % 2
    me = ep * 2 + sub
    rows, heads, hd = q_ref.shape
    half = rows // 2
    experts, width, ff = g_hbm.shape
    window = k_s.shape[1]

    def at(z, y, c):
        return {"ep": z * 2 + y, "sub": c}

    def remote(src, dst, ss, rs, where):
        return pltpu.make_async_remote_copy(
            src_ref=src, dst_ref=dst, send_sem=ss, recv_sem=rs,
            device_id=where, device_id_type=MESH,
        )

    k_cp = pltpu.make_async_copy(k_hbm, k_s, load_sem.at[0])
    v_cp = pltpu.make_async_copy(v_hbm, v_s, load_sem.at[1])
    op_cp = pltpu.make_async_copy(op_hbm, op_s, load_sem.at[2])
    k_cp.start()
    v_cp.start()
    op_cp.start()

    barrier = pltpu.get_barrier_semaphore()
    for k in range(1, n):
        peer = (me + k) % n
        pl.semaphore_signal(barrier, inc=1, device_id={"ep": peer // 2, "sub": peer % 2}, device_id_type=MESH)
    pl.semaphore_wait(barrier, n - 1)

    ids = lax.broadcasted_iota(jnp.int32, (128, half), 0)
    dense = jnp.zeros((128, half), F32)
    for t in range(route_ref.shape[0]):
        dense = dense + jnp.where(route_ref[t : t + 1, :] == ids, rw_ref[t : t + 1, :], 0.0)
    w_row[...] = jnp.zeros_like(w_row)
    w_row[0:128, 0:half] = dense
    w_own[...] = w_row[0:128, 0:128].T[0:PAD]
    w_all[sub, lo, hi] = w_own[...]
    w_copies = []
    for k in range(1, n):
        peer = (me + k) % n
        cp = remote(w_own, w_all.at[sub, lo, hi], ws_sem.at[k], wr_sem.at[k], {"ep": peer // 2, "sub": peer % 2})
        cp.start()
        w_copies.append(cp)

    ho[...] = jnp.zeros_like(ho)
    k_cp.wait()
    v_cp.wait()
    for e in range(experts):
        pltpu.make_async_copy(g_hbm.at[e], g_s.at[e], g_sem.at[e]).start()
        pltpu.make_async_copy(u_hbm.at[e], u_s.at[e], u_sem.at[e]).start()
    for e in range(experts):
        pltpu.make_async_copy(d_hbm.at[e], d_s.at[e], d_sem.at[e]).start()
    nk[...] = nk_ref[...].astype(F32)
    nv[...] = nv_ref[...].astype(F32)

    scale = 1.0 / math.sqrt(hd)
    slots = lax.broadcasted_iota(jnp.int32, (heads, window), 1)

    def attend(i, carry):
        bs = [i * unroll + j for j in range(unroll)]
        qs = [q_ref[b] for b in bs]
        ss = [
            lax.dot_general(q, k_s[b], (((1,), (1,)), ((), ())), preferred_element_type=F32) * scale
            for q, b in zip(qs, bs)
        ]
        owns = [
            jnp.sum(q.astype(F32) * nk[pl.ds(b, 1), :], -1, keepdims=True) * scale for q, b in zip(qs, bs)
        ]
        ss = [jnp.where(slots < len_ref[b], s, -1e30) for s, b in zip(ss, bs)]
        tops = [jnp.maximum(jnp.max(s, -1, keepdims=True), o) for s, o in zip(ss, owns)]
        ws = [jnp.exp(s - t) for s, t in zip(ss, tops)]
        os = [jnp.exp(o - t) for o, t in zip(owns, tops)]
        dens = [jnp.sum(w, -1, keepdims=True) + o for w, o in zip(ws, os)]
        mixes = [
            jnp.dot(w.astype(BF16), v_s[b], preferred_element_type=F32)
            + o.astype(BF16).astype(F32) * nv[pl.ds(b, 1), :]
            for w, o, b in zip(ws, os, bs)
        ]
        for m, d, b in zip(mixes, dens, bs):
            ho[(b // half) * PAD + b % half] = m / d
        return carry

    lax.fori_loop(0, rows // unroll, attend, 0)

    flat = jnp.concatenate([ho[:, h, :] for h in range(heads)], axis=1).astype(BF16)
    op_cp.wait()
    piece = width // CHUNKS

    def project(j, carry):
        cols = pl.ds(pl.multiple_of(j * piece, piece), piece)
        p = jnp.dot(flat, op_s[:, cols], preferred_element_type=F32)
        pr[0, :, cols] = p[:PAD]
        pr[1, :, cols] = p[PAD:]
        return carry

    lax.fori_loop(0, CHUNKS, project, 0)
    pr_cp = remote(pr.at[1 - sub], prr, pr_sem.at[0], pr_sem.at[1], at(hi, lo, 1 - sub))
    pr_cp.start()
    pr_cp.wait()
    stream[...] = pr[sub] + prr[...]
    stream[0:half, :] = stream[0:half, :] + res_ref[...].astype(F32)
    x = stream[...]
    normed = x * lax.rsqrt(jnp.mean(x * x, -1, keepdims=True) + 1e-6) * gain_ref[...]
    cut = width // PARTS
    for p in range(PARTS):
        xa[p, sub, lo, hi] = normed[:, p * cut : (p + 1) * cut].astype(BF16)

    sends = []

    def go(src, ss, rs, where):
        cp = remote(src, src, ss, rs, where)
        cp.start()
        sends.append(cp)

    for p in range(PARTS):
        own = xa.at[p, sub, lo, hi]
        for k in range(1, nz):
            go(own, zs_sem.at[p, k], zr_sem.at[p, k], at((hi + k) % nz, lo, sub))
        go(own, ys_sem.at[p, 0], yr_sem.at[p, 0], at(hi, 1 - lo, sub))
        go(own, cs_sem.at[p, 0, 0], cr_sem.at[p, 0, 0], at(hi, lo, 1 - sub))

    def landed(p, c, y, k, rs):
        ref = xa.at[p, c, y, (hi - k + nz) % nz]
        remote(ref, ref, rs, rs, at(hi, lo, 1 - sub)).wait_recv()
        return ref

    for p in range(PARTS):
        for k in range(1, nz):
            ref = landed(p, sub, lo, k, zr_sem.at[p, k])
            go(ref, ys_sem.at[p, k], yr_sem.at[p, k], at(hi, 1 - lo, sub))
            go(ref, cs_sem.at[p, 0, k], cr_sem.at[p, 0, k], at(hi, lo, 1 - sub))
    for p in range(PARTS):
        for k in range(nz):
            ref = landed(p, sub, 1 - lo, k, yr_sem.at[p, k])
            go(ref, cs_sem.at[p, 1, k], cr_sem.at[p, 1, k], at(hi, lo, 1 - sub))
    for p in range(PARTS):
        for k in range(nz):
            landed(p, 1 - sub, lo, k, cr_sem.at[p, 0, k])
            landed(p, 1 - sub, 1 - lo, k, cr_sem.at[p, 1, k])
    for cp in w_copies:
        cp.wait()

    total = n * half
    slots_all = n * PAD
    r_id = lax.broadcasted_iota(jnp.int32, (total, slots_all), 0)
    p_id = lax.broadcasted_iota(jnp.int32, (total, slots_all), 1)
    pick = ((p_id // PAD) * half + p_id % PAD == r_id) & (p_id % PAD < half)
    pick = jnp.where(pick, 1.0, 0.0).astype(BF16)
    for p in range(PARTS):
        packed = jnp.dot(pick, xa[p].reshape(slots_all, cut), preferred_element_type=F32)
        xc[:, p * cut : (p + 1) * cut] = packed.astype(BF16)
    for c in range(2):
        for y in range(2):
            for z in range(nz):
                at_row = ((c * 2 + y) * nz + z) * half
                w_row[at_row : at_row + half, :] = w_all[c, y, z, 0:half, :]
    tiles = ff // TILE
    lane = lax.broadcasted_iota(jnp.int32, (total, 128), 1)

    def expert(e, carry):
        pltpu.make_async_copy(g_hbm.at[e], g_s.at[e], g_sem.at[e]).wait()
        pltpu.make_async_copy(u_hbm.at[e], u_s.at[e], u_sem.at[e]).wait()
        w_e = jnp.sum(jnp.where(lane == me * experts + e, w_row[0:total, :], 0.0), -1, keepdims=True)

        def tile(t, carry):
            cols = pl.ds(pl.multiple_of(t * TILE, TILE), TILE)
            xs = xc[...]
            g = jnp.dot(xs, g_s[e, :, cols], preferred_element_type=F32)
            u = jnp.dot(xs, u_s[e, :, cols], preferred_element_type=F32)
            h = (g / (1.0 + jnp.exp(-g))) * u * w_e
            hid[:, pl.ds(pl.multiple_of(e * ff + t * TILE, TILE), TILE)] = h.astype(BF16)
            return carry

        return lax.fori_loop(0, tiles, tile, carry)

    lax.fori_loop(0, experts, expert, 0)
    for e in range(experts):
        pltpu.make_async_copy(d_hbm.at[e], d_s.at[e], d_sem.at[e]).wait()

    firsts, seconds, thirds = {}, {}, {}
    quarter = nz * half
    wide = s1.shape[2]

    def spread(groups, step, wider):
        shape = (groups * wider, groups * step)
        o_id = lax.broadcasted_iota(jnp.int32, shape, 0)
        i_id = lax.broadcasted_iota(jnp.int32, shape, 1)
        hit = ((o_id // wider) * step + o_id % wider == i_id) & (o_id % wider < step)
        return jnp.where(hit, 1.0, 0.0).astype(BF16)

    by_y, by_z = spread(2, quarter, wide), spread(nz, half, PAD)

    def down(j):
        acc = jnp.dot(
            hid[...],
            d_s[:, :, j * piece : (j + 1) * piece].reshape(experts * ff, piece),
            preferred_element_type=F32,
        )
        part[j] = acc.astype(BF16).reshape(2, 2 * quarter, piece)
        firsts[j] = remote(part.at[j, 1 - sub], r1.at[j], a_send.at[j], a_recv.at[j], at(hi, lo, 1 - sub))
        firsts[j].start()

    def second(j):
        firsts[j].wait()
        both = (part[j, sub].astype(F32) + r1[j].astype(F32)).astype(BF16)
        s1[j] = jnp.dot(by_y, both, preferred_element_type=F32).astype(BF16).reshape(2, wide, piece)
        seconds[j] = remote(s1.at[j, 1 - lo], r2.at[j], b_send.at[j], b_recv.at[j], at(hi, 1 - lo, sub))
        seconds[j].start()

    def third(j):
        seconds[j].wait()
        both = (s1[j, lo].astype(F32) + r2[j].astype(F32))[:quarter].astype(BF16)
        s2[j] = jnp.dot(by_z, both, preferred_element_type=F32).astype(BF16).reshape(nz, PAD, piece)
        thirds[j] = []
        for k in range(1, nz):
            z = (hi + k) % nz
            cp = remote(s2.at[j, z], r3.at[j, k], c_send.at[j, k], c_recv.at[j, k], at(z, lo, sub))
            cp.start()
            thirds[j].append(cp)

    def final(j):
        acc = s2[j, hi].astype(F32)
        for k in range(1, nz):
            thirds[j][k - 1].wait()
            acc = acc + r3[j, k].astype(F32)
        acc = acc + stream[:, j * piece : (j + 1) * piece]
        out_ref[:, j * piece : (j + 1) * piece] = acc[:half].astype(out_ref.dtype)

    for step in range(CHUNKS + 3):
        if step < CHUNKS:
            down(step)
        for lag, stage in ((1, second), (2, third), (3, final)):
            if 0 <= step - lag < CHUNKS:
                stage(step - lag)
    for cp in sends:
        cp.wait_send()


def per_device(
    queries, cache_keys, cache_values, new_keys, new_values, lengths, out_proj, residual,
    norm_gain, gate_proj, up_proj, down_proj, routing, route_weights,
):
    n_ep = lax.axis_size("ep")
    rows, heads, hd = queries.shape
    window = cache_keys.shape[2]
    half, width = residual.shape
    experts, _, ff = gate_proj.shape
    nz, n = n_ep // 2, n_ep * 2
    piece = width // CHUNKS
    wide = -(-nz * half // PAD) * PAD
    unroll = next(u for u in (5, 4, 2, 1) if rows % u == 0)
    vmem = pl.BlockSpec(memory_space=pltpu.VMEM)
    hbm = pl.BlockSpec(memory_space=pl.ANY)
    dma = pltpu.SemaphoreType.DMA
    return pl.pallas_call(
        functools.partial(kernel, n_ep, unroll),
        out_shape=jax.ShapeDtypeStruct((half, width), BF16),
        in_specs=[vmem] * 3 + [pl.BlockSpec(memory_space=pltpu.SMEM)] + [vmem] * 4 + [hbm] * 6,
        out_specs=vmem,
        scratch_shapes=[
            pltpu.VMEM((rows, window, hd), BF16),
            pltpu.VMEM((rows, window, hd), BF16),
            pltpu.VMEM(out_proj.shape, BF16),
            pltpu.VMEM(gate_proj.shape, BF16),
            pltpu.VMEM(up_proj.shape, BF16),
            pltpu.VMEM(down_proj.shape, BF16),
            pltpu.VMEM((2 * PAD, heads, hd), F32),
            pltpu.VMEM((2, PAD, width), F32),
            pltpu.VMEM((PAD, width), F32),
            pltpu.VMEM((PAD, width), F32),
            pltpu.VMEM((PAD, 128), F32),
            pltpu.VMEM((2, 2, nz, PAD, 128), F32),
            pltpu.VMEM((max(128, n * half), 128), F32),
            pltpu.VMEM((rows, hd), F32),
            pltpu.VMEM((rows, hd), F32),
            pltpu.VMEM((PARTS, 2, 2, nz, PAD, width // PARTS), BF16),
            pltpu.VMEM((n * half, width), BF16),
            pltpu.VMEM((n * half, experts * ff), BF16),
            pltpu.VMEM((CHUNKS, 2, n_ep * half, piece), BF16),
            pltpu.VMEM((CHUNKS, n_ep * half, piece), BF16),
            pltpu.VMEM((CHUNKS, 2, wide, piece), BF16),
            pltpu.VMEM((CHUNKS, wide, piece), BF16),
            pltpu.VMEM((CHUNKS, nz, PAD, piece), BF16),
            pltpu.VMEM((CHUNKS, nz, PAD, piece), BF16),
            dma((3,)), dma((experts,)), dma((experts,)), dma((experts,)), dma((2,)), dma((n,)), dma((n,)),
            dma((PARTS, nz)), dma((PARTS, nz)), dma((PARTS, nz)), dma((PARTS, nz)), dma((PARTS, 2, nz)), dma((PARTS, 2, nz)),
            dma((CHUNKS,)), dma((CHUNKS,)), dma((CHUNKS,)), dma((CHUNKS,)), dma((CHUNKS, nz)), dma((CHUNKS, nz)),
        ],
        compiler_params=pltpu.CompilerParams(
            collective_id=0, has_side_effects=True, vmem_limit_bytes=60 * 1024 * 1024
        ),
    )(
        queries, new_keys.transpose(1, 0, 2).reshape(rows, hd), new_values.transpose(1, 0, 2).reshape(rows, hd),
        lengths, residual, norm_gain.reshape(1, width), routing.T, route_weights.T,
        cache_keys.reshape(rows, window, hd), cache_values.reshape(rows, window, hd), out_proj,
        gate_proj, up_proj, down_proj,
    )


def solution(mesh):
    return jax.shard_map(
        per_device,
        mesh=mesh,
        in_specs=(
            P(("grp", "ep"), "sub", None),
            P(("grp", "ep"), "sub", None, None),
            P(("grp", "ep"), "sub", None, None),
            P(("grp", "ep"), "sub", None),
            P(("grp", "ep"), "sub", None),
            P(("grp", "ep")),
            P("sub", None),
            P(("grp", "ep", "sub"), None),
            P(),
            P(("ep", "sub"), None, None),
            P(("ep", "sub"), None, None),
            P(("ep", "sub"), None, None),
            P(("grp", "ep", "sub"), None),
            P(("grp", "ep", "sub"), None),
        ),
        out_specs=P(("grp", "ep", "sub"), None),
        check_vma=False,
    )
```

```python
import functools
import math

import jax
import jax.numpy as jnp
from jax import lax
from jax.experimental import pallas as pl
from jax.experimental.pallas import tpu as pltpu
from jax.sharding import PartitionSpec as P

PAD = 16
CHUNKS = 2
PARTS = 2
TILE = 256
MESH = pl.DeviceIdType.MESH
F32 = jnp.float32
BF16 = jnp.bfloat16


def kernel(
    n_ep, unroll,
    q_ref, nk_ref, nv_ref, len_ref, res_ref, gain_ref, route_ref, rw_ref,
    k_hbm, v_hbm, op_hbm, g_hbm, u_hbm, d_hbm,
    out_ref,
    k_s, v_s, op_s, g_s, u_s, d_s,
    ho, pr, prr, stream, w_own, w_all, w_row, nk, nv, xa, xc, hid, part, r1, s1, r2, s2, r3,
    load_sem, g_sem, u_sem, d_sem, pr_sem, ws_sem, wr_sem,
    zs_sem, zr_sem, ys_sem, yr_sem, cs_sem, cr_sem,
    a_send, a_recv, b_send, b_recv, c_send, c_recv,
):
    nz = n_ep // 2
    n = n_ep * 2
    ep, sub = lax.axis_index("ep"), lax.axis_index("sub")
    hi, lo = ep // 2, ep % 2
    me = ep * 2 + sub
    rows, heads, hd = q_ref.shape
    half = rows // 2
    experts, width, ff = g_hbm.shape
    window = k_s.shape[1]

    def at(z, y, c):
        return {"ep": z * 2 + y, "sub": c}

    def remote(src, dst, ss, rs, where):
        return pltpu.make_async_remote_copy(
            src_ref=src, dst_ref=dst, send_sem=ss, recv_sem=rs,
            device_id=where, device_id_type=MESH,
        )

    k_cp = pltpu.make_async_copy(k_hbm, k_s, load_sem.at[0])
    v_cp = pltpu.make_async_copy(v_hbm, v_s, load_sem.at[1])
    op_cp = pltpu.make_async_copy(op_hbm, op_s, load_sem.at[2])
    k_cp.start()
    v_cp.start()
    op_cp.start()

    barrier = pltpu.get_barrier_semaphore()
    for k in range(1, n):
        peer = (me + k) % n
        pl.semaphore_signal(barrier, inc=1, device_id={"ep": peer // 2, "sub": peer % 2}, device_id_type=MESH)
    pl.semaphore_wait(barrier, n - 1)

    ids = lax.broadcasted_iota(jnp.int32, (128, half), 0)
    dense = jnp.zeros((128, half), F32)
    for t in range(route_ref.shape[0]):
        dense = dense + jnp.where(route_ref[t : t + 1, :] == ids, rw_ref[t : t + 1, :], 0.0)
    w_row[...] = jnp.zeros_like(w_row)
    w_row[0:128, 0:half] = dense
    w_own[...] = w_row[0:128, 0:128].T[0:PAD]
    w_all[sub, lo, hi] = w_own[...]
    w_copies = []
    for k in range(1, n):
        peer = (me + k) % n
        cp = remote(w_own, w_all.at[sub, lo, hi], ws_sem.at[k], wr_sem.at[k], {"ep": peer // 2, "sub": peer % 2})
        cp.start()
        w_copies.append(cp)

    ho[...] = jnp.zeros_like(ho)
    k_cp.wait()
    v_cp.wait()
    for e in range(experts):
        pltpu.make_async_copy(g_hbm.at[e], g_s.at[e], g_sem.at[e]).start()
        pltpu.make_async_copy(u_hbm.at[e], u_s.at[e], u_sem.at[e]).start()
    for e in range(experts):
        pltpu.make_async_copy(d_hbm.at[e], d_s.at[e], d_sem.at[e]).start()
    nk[...] = nk_ref[...].astype(F32)
    nv[...] = nv_ref[...].astype(F32)

    scale = 1.0 / math.sqrt(hd)
    slots = lax.broadcasted_iota(jnp.int32, (heads, window), 1)

    def attend(i, carry):
        bs = [i * unroll + j for j in range(unroll)]
        qs = [q_ref[b] for b in bs]
        ss = [
            lax.dot_general(q, k_s[b], (((1,), (1,)), ((), ())), preferred_element_type=F32) * scale
            for q, b in zip(qs, bs)
        ]
        owns = [
            jnp.sum(q.astype(F32) * nk[pl.ds(b, 1), :], -1, keepdims=True) * scale for q, b in zip(qs, bs)
        ]
        ss = [jnp.where(slots < len_ref[b], s, -1e30) for s, b in zip(ss, bs)]
        tops = [jnp.maximum(jnp.max(s, -1, keepdims=True), o) for s, o in zip(ss, owns)]
        ws = [jnp.exp(s - t) for s, t in zip(ss, tops)]
        os = [jnp.exp(o - t) for o, t in zip(owns, tops)]
        dens = [jnp.sum(w, -1, keepdims=True) + o for w, o in zip(ws, os)]
        mixes = [
            jnp.dot(w.astype(BF16), v_s[b], preferred_element_type=F32)
            + o.astype(BF16).astype(F32) * nv[pl.ds(b, 1), :]
            for w, o, b in zip(ws, os, bs)
        ]
        for m, d, b in zip(mixes, dens, bs):
            ho[(b // half) * PAD + b % half] = m / d
        return carry

    lax.fori_loop(0, rows // unroll, attend, 0)

    flat = jnp.concatenate([ho[:, h, :] for h in range(heads)], axis=1).astype(BF16)
    op_cp.wait()
    piece = width // CHUNKS

    def project(j, carry):
        cols = pl.ds(pl.multiple_of(j * piece, piece), piece)
        p = jnp.dot(flat, op_s[:, cols], preferred_element_type=F32)
        pr[0, :, cols] = p[:PAD]
        pr[1, :, cols] = p[PAD:]
        return carry

    lax.fori_loop(0, CHUNKS, project, 0)
    pr_cp = remote(pr.at[1 - sub], prr, pr_sem.at[0], pr_sem.at[1], at(hi, lo, 1 - sub))
    pr_cp.start()
    pr_cp.wait()
    stream[...] = pr[sub] + prr[...]
    stream[0:half, :] = stream[0:half, :] + res_ref[...].astype(F32)
    x = stream[...]
    normed = x * lax.rsqrt(jnp.mean(x * x, -1, keepdims=True) + 1e-6) * gain_ref[...]
    cut = width // PARTS
    for p in range(PARTS):
        xa[p, sub, lo, hi] = normed[:, p * cut : (p + 1) * cut].astype(BF16)

    sends = []

    def go(src, ss, rs, where):
        cp = remote(src, src, ss, rs, where)
        cp.start()
        sends.append(cp)

    for p in range(PARTS):
        own = xa.at[p, sub, lo, hi]
        for k in range(1, nz):
            go(own, zs_sem.at[p, k], zr_sem.at[p, k], at((hi + k) % nz, lo, sub))
        go(own, ys_sem.at[p, 0], yr_sem.at[p, 0], at(hi, 1 - lo, sub))
        go(own, cs_sem.at[p, 0, 0], cr_sem.at[p, 0, 0], at(hi, lo, 1 - sub))

    def landed(p, c, y, k, rs):
        ref = xa.at[p, c, y, (hi - k + nz) % nz]
        remote(ref, ref, rs, rs, at(hi, lo, 1 - sub)).wait_recv()
        return ref

    def across(p, k):
        ref = landed(p, sub, 1 - lo, k, yr_sem.at[p, k])
        go(ref, cs_sem.at[p, 1, k], cr_sem.at[p, 1, k], at(hi, lo, 1 - sub))

    for p in range(PARTS):
        for k in range(1, nz):
            ref = landed(p, sub, lo, k, zr_sem.at[p, k])
            go(ref, ys_sem.at[p, k], yr_sem.at[p, k], at(hi, 1 - lo, sub))
            go(ref, cs_sem.at[p, 0, k], cr_sem.at[p, 0, k], at(hi, lo, 1 - sub))
            across(p, k - 1)
    for p in range(PARTS):
        across(p, nz - 1)
    for p in range(PARTS):
        for k in range(nz):
            landed(p, 1 - sub, lo, k, cr_sem.at[p, 0, k])
            landed(p, 1 - sub, 1 - lo, k, cr_sem.at[p, 1, k])
    for cp in w_copies:
        cp.wait()

    total = n * half
    slots_all = n * PAD
    r_id = lax.broadcasted_iota(jnp.int32, (total, slots_all), 0)
    p_id = lax.broadcasted_iota(jnp.int32, (total, slots_all), 1)
    pick = ((p_id // PAD) * half + p_id % PAD == r_id) & (p_id % PAD < half)
    pick = jnp.where(pick, 1.0, 0.0).astype(BF16)
    for p in range(PARTS):
        packed = jnp.dot(pick, xa[p].reshape(slots_all, cut), preferred_element_type=F32)
        xc[:, p * cut : (p + 1) * cut] = packed.astype(BF16)
    for c in range(2):
        for y in range(2):
            for z in range(nz):
                at_row = ((c * 2 + y) * nz + z) * half
                w_row[at_row : at_row + half, :] = w_all[c, y, z, 0:half, :]
    tiles = ff // TILE
    lane = lax.broadcasted_iota(jnp.int32, (total, 128), 1)

    def expert(e, carry):
        pltpu.make_async_copy(g_hbm.at[e], g_s.at[e], g_sem.at[e]).wait()
        pltpu.make_async_copy(u_hbm.at[e], u_s.at[e], u_sem.at[e]).wait()
        w_e = jnp.sum(jnp.where(lane == me * experts + e, w_row[0:total, :], 0.0), -1, keepdims=True)

        def tile(t, carry):
            cols = pl.ds(pl.multiple_of(t * TILE, TILE), TILE)
            xs = xc[...]
            g = jnp.dot(xs, g_s[e, :, cols], preferred_element_type=F32)
            u = jnp.dot(xs, u_s[e, :, cols], preferred_element_type=F32)
            h = (g / (1.0 + jnp.exp(-g))) * u * w_e
            hid[:, pl.ds(pl.multiple_of(e * ff + t * TILE, TILE), TILE)] = h.astype(BF16)
            return carry

        return lax.fori_loop(0, tiles, tile, carry)

    lax.fori_loop(0, experts, expert, 0)
    for e in range(experts):
        pltpu.make_async_copy(d_hbm.at[e], d_s.at[e], d_sem.at[e]).wait()

    firsts, seconds, thirds = {}, {}, {}
    quarter = nz * half
    wide = s1.shape[2]

    def spread(groups, step, wider):
        shape = (groups * wider, groups * step)
        o_id = lax.broadcasted_iota(jnp.int32, shape, 0)
        i_id = lax.broadcasted_iota(jnp.int32, shape, 1)
        hit = ((o_id // wider) * step + o_id % wider == i_id) & (o_id % wider < step)
        return jnp.where(hit, 1.0, 0.0).astype(BF16)

    by_y, by_z = spread(2, quarter, wide), spread(nz, half, PAD)

    def down(j):
        acc = jnp.dot(
            hid[...],
            d_s[:, :, j * piece : (j + 1) * piece].reshape(experts * ff, piece),
            preferred_element_type=F32,
        )
        part[j] = acc.astype(BF16).reshape(2, 2 * quarter, piece)
        firsts[j] = remote(part.at[j, 1 - sub], r1.at[j], a_send.at[j], a_recv.at[j], at(hi, lo, 1 - sub))
        firsts[j].start()

    def second(j):
        firsts[j].wait()
        both = (part[j, sub].astype(F32) + r1[j].astype(F32)).astype(BF16)
        s1[j] = jnp.dot(by_y, both, preferred_element_type=F32).astype(BF16).reshape(2, wide, piece)
        seconds[j] = remote(s1.at[j, 1 - lo], r2.at[j], b_send.at[j], b_recv.at[j], at(hi, 1 - lo, sub))
        seconds[j].start()

    def third(j):
        seconds[j].wait()
        both = (s1[j, lo].astype(F32) + r2[j].astype(F32))[:quarter].astype(BF16)
        s2[j] = jnp.dot(by_z, both, preferred_element_type=F32).astype(BF16).reshape(nz, PAD, piece)
        thirds[j] = []
        for k in range(1, nz):
            z = (hi + k) % nz
            cp = remote(s2.at[j, z], r3.at[j, k], c_send.at[j, k], c_recv.at[j, k], at(z, lo, sub))
            cp.start()
            thirds[j].append(cp)

    def final(j):
        acc = s2[j, hi].astype(F32)
        for k in range(1, nz):
            thirds[j][k - 1].wait()
            acc = acc + r3[j, k].astype(F32)
        acc = acc + stream[:, j * piece : (j + 1) * piece]
        out_ref[:, j * piece : (j + 1) * piece] = acc[:half].astype(out_ref.dtype)

    for step in range(CHUNKS + 3):
        if step < CHUNKS:
            down(step)
        for lag, stage in ((1, second), (2, third), (3, final)):
            if 0 <= step - lag < CHUNKS:
                stage(step - lag)
    for cp in sends:
        cp.wait_send()


def per_device(
    queries, cache_keys, cache_values, new_keys, new_values, lengths, out_proj, residual,
    norm_gain, gate_proj, up_proj, down_proj, routing, route_weights,
):
    n_ep = lax.axis_size("ep")
    rows, heads, hd = queries.shape
    window = cache_keys.shape[2]
    half, width = residual.shape
    experts, _, ff = gate_proj.shape
    nz, n = n_ep // 2, n_ep * 2
    piece = width // CHUNKS
    wide = -(-nz * half // PAD) * PAD
    unroll = next(u for u in (5, 4, 2, 1) if rows % u == 0)
    vmem = pl.BlockSpec(memory_space=pltpu.VMEM)
    hbm = pl.BlockSpec(memory_space=pl.ANY)
    dma = pltpu.SemaphoreType.DMA
    return pl.pallas_call(
        functools.partial(kernel, n_ep, unroll),
        out_shape=jax.ShapeDtypeStruct((half, width), BF16),
        in_specs=[vmem] * 3 + [pl.BlockSpec(memory_space=pltpu.SMEM)] + [vmem] * 4 + [hbm] * 6,
        out_specs=vmem,
        scratch_shapes=[
            pltpu.VMEM((rows, window, hd), BF16),
            pltpu.VMEM((rows, window, hd), BF16),
            pltpu.VMEM(out_proj.shape, BF16),
            pltpu.VMEM(gate_proj.shape, BF16),
            pltpu.VMEM(up_proj.shape, BF16),
            pltpu.VMEM(down_proj.shape, BF16),
            pltpu.VMEM((2 * PAD, heads, hd), F32),
            pltpu.VMEM((2, PAD, width), F32),
            pltpu.VMEM((PAD, width), F32),
            pltpu.VMEM((PAD, width), F32),
            pltpu.VMEM((PAD, 128), F32),
            pltpu.VMEM((2, 2, nz, PAD, 128), F32),
            pltpu.VMEM((max(128, n * half), 128), F32),
            pltpu.VMEM((rows, hd), F32),
            pltpu.VMEM((rows, hd), F32),
            pltpu.VMEM((PARTS, 2, 2, nz, PAD, width // PARTS), BF16),
            pltpu.VMEM((n * half, width), BF16),
            pltpu.VMEM((n * half, experts * ff), BF16),
            pltpu.VMEM((CHUNKS, 2, n_ep * half, piece), BF16),
            pltpu.VMEM((CHUNKS, n_ep * half, piece), BF16),
            pltpu.VMEM((CHUNKS, 2, wide, piece), BF16),
            pltpu.VMEM((CHUNKS, wide, piece), BF16),
            pltpu.VMEM((CHUNKS, nz, PAD, piece), BF16),
            pltpu.VMEM((CHUNKS, nz, PAD, piece), BF16),
            dma((3,)), dma((experts,)), dma((experts,)), dma((experts,)), dma((2,)), dma((n,)), dma((n,)),
            dma((PARTS, nz)), dma((PARTS, nz)), dma((PARTS, nz)), dma((PARTS, nz)), dma((PARTS, 2, nz)), dma((PARTS, 2, nz)),
            dma((CHUNKS,)), dma((CHUNKS,)), dma((CHUNKS,)), dma((CHUNKS,)), dma((CHUNKS, nz)), dma((CHUNKS, nz)),
        ],
        compiler_params=pltpu.CompilerParams(
            collective_id=0, has_side_effects=True, vmem_limit_bytes=60 * 1024 * 1024
        ),
    )(
        queries, new_keys.transpose(1, 0, 2).reshape(rows, hd), new_values.transpose(1, 0, 2).reshape(rows, hd),
        lengths, residual, norm_gain.reshape(1, width), routing.T, route_weights.T,
        cache_keys.reshape(rows, window, hd), cache_values.reshape(rows, window, hd), out_proj,
        gate_proj, up_proj, down_proj,
    )


def solution(mesh):
    return jax.shard_map(
        per_device,
        mesh=mesh,
        in_specs=(
            P(("grp", "ep"), "sub", None),
            P(("grp", "ep"), "sub", None, None),
            P(("grp", "ep"), "sub", None, None),
            P(("grp", "ep"), "sub", None),
            P(("grp", "ep"), "sub", None),
            P(("grp", "ep")),
            P("sub", None),
            P(("grp", "ep", "sub"), None),
            P(),
            P(("ep", "sub"), None, None),
            P(("ep", "sub"), None, None),
            P(("ep", "sub"), None, None),
            P(("grp", "ep", "sub"), None),
            P(("grp", "ep", "sub"), None),
        ),
        out_specs=P(("grp", "ep", "sub"), None),
        check_vma=False,
    )
```
